128 devices in a mesh: ctx: 8 (over x, z_hi), grp: 16 (over y, z_lo, core).
Axes of the slice: x: 4, y: 4, z: 4 (z_hi: 2, z_lo: 2; z = z_hi * 2 + z_lo), core: 2. Of those that a mesh axis runs over, the one named last changes fastest.
Arguments:
- tail_q: bfloat16 [16, 512, 8192], P('grp', 'ctx'), may hold values from -6 to 6
- prompt_kv: bfloat16 [16, 4480, 2048], P('grp', 'ctx'), may hold values from -6 to 6
- dest_owner: int32 [16, 8, 35, 1], P('grp', 'ctx'), may hold values from 0 to 15; in each aligned block of 35 rows (0 to 34, 35 to 69, ..., all dimensions but the last counted through in order) at most 5 rows name the same one
- dest_row: int32 [16, 8, 35], P('grp', 'ctx'), may hold values from 0 to 3
- dec_q: bfloat16 [64, 2, 8192], P('grp'), may hold values from -6 to 6
- new_kv: bfloat16 [64, 2, 2048], P('grp'), may hold values from -6 to 6
- res_kv: bfloat16 [64, 1024, 2048], P('grp', 'ctx'), may hold values from -6 to 6
- lens: int32 [64], P('grp'), may hold values from 1 to 1024, 32768 in all
Outputs:
- prefill_out: bfloat16 [16, 512, 8192], P('grp', 'ctx')
- decode_out: bfloat16 [64, 2, 8192], P('grp', None, 'ctx')
The draws below stay inside these ranges and needn't reach their ends.
Inputs may be any that keep to these rules, and one draw needn't show every extreme that they name: `dest_owner`: among the 35 blocks of one prompt shard (one device), no owner is named more than 5 times; in some shards one owner is named exactly 5 times.
All inputs are finite; a program needn't handle non-finite values. No bound on the sum of `lens` on one device may be relied on, other than what follows from the above.
Results may differ from the reference program's by a relative error of at most 0.012.
Values may be sent and summed in bfloat16 or wider, within the bound.
No kernel may reach another device: no remote copies, remote signals or barrier semaphores. Data moves between devices by JAX's collectives and lax.ppermute only.
A program may use at most 128 MiB of HBM per device.

```python
import math
import jax
import jax.numpy as jnp
import numpy as np
from jax import lax

KVH = 8
HD = 128
PRE_DEV = 496
TAIL_DEV = 64
BLK = 16
ROW_GRP = 4
GROUP = 8
KVD = 1024
QD = 8192
SEQ_DEV = 560
NB = 35
CAP = 5
PROMPT = 4480
TAIL = 512
RES = 1024
ROWS = 64
N_CTX = 8
N_GRP = 16


def draw_tail_q(key, part):
    key = jax.random.fold_in(key, 1)
    shape = (N_GRP, TAIL, QD)
    values = jnp.clip(jax.random.normal(key, shape, jnp.float32), -6.0, 6.0)
    return values.astype(jnp.bfloat16)


def draw_prompt_kv(key, part):
    key = jax.random.fold_in(key, 2)
    shape = (N_GRP, PROMPT, 2 * KVD)
    values = jnp.clip(jax.random.normal(key, shape, jnp.float32), -6.0, 6.0)
    return values.astype(jnp.bfloat16)


def draw_dec_q(key, part):
    key = jax.random.fold_in(key, 3)
    shape = (ROWS, 2, QD)
    values = jnp.clip(jax.random.normal(key, shape, jnp.float32), -6.0, 6.0)
    return values.astype(jnp.bfloat16)


def draw_new_kv(key, part):
    key = jax.random.fold_in(key, 4)
    shape = (ROWS, 2, 2 * KVD)
    values = jnp.clip(jax.random.normal(key, shape, jnp.float32), -6.0, 6.0)
    return values.astype(jnp.bfloat16)


def draw_res_kv(key, part):
    key = jax.random.fold_in(key, 5)
    shape = (ROWS, RES, 2 * KVD)
    values = jnp.clip(jax.random.normal(key, shape, jnp.float32), -6.0, 6.0)
    return values.astype(jnp.bfloat16)


def set_ends(drawn, rng, low, largest):
    place = [jax.random.randint(jax.random.fold_in(rng, axis), (), 0, length) for axis, length in enumerate(drawn.shape)]
    main_axis = drawn.shape.index(max(drawn.shape))
    next_to = place[:main_axis] + [(place[main_axis] + 1) % drawn.shape[main_axis]] + place[main_axis + 1:]
    return drawn.at[tuple(place)].set(low).at[tuple(next_to)].set(largest)


def split_up(number_of, total, reach, slope):
    loads = [(1 << 20) // math.isqrt(rank ** slope) + 1 for rank in range(2, number_of + 1)]
    surplus, counts = total - reach - (number_of - 1), [1] * (number_of - 1)
    while surplus > 0:
        movable = [i for i in range(number_of - 1) if counts[i] < reach]
        mass, left = sum([loads[i] for i in movable]), surplus
        for i in movable:
            addition = min(reach - counts[i], max(1, left * loads[i] // mass), surplus)
            counts[i] = counts[i] + addition
            surplus = surplus - addition
    return np.array([reach] + counts)


def uneven(stream_key, amount, total, bound, lean):
    if amount == 2:
        one = jax.random.randint(stream_key, (), max(1, total - bound), min(bound, total - 1) + 1)
        return jnp.stack([one, total - one])
    sizes = jnp.asarray(split_up(amount, total, bound, lean), jnp.int32)
    twos = (amount - 1) // 2
    donor, receiver = sizes[1:1 + 2 * twos:2], sizes[2:2 + 2 * twos:2]
    margin = jnp.minimum(donor - 1, bound - receiver)
    shifted = jax.random.randint(jax.random.fold_in(stream_key, 1), (twos,), 0, 1 << 20) % (margin + 1)
    sizes = sizes.at[1:1 + 2 * twos:2].set(donor - shifted).at[2:2 + 2 * twos:2].set(receiver + shifted)
    return sizes[jax.random.permutation(jax.random.fold_in(stream_key, 2), amount)]


def shared_out(stream_key, own, number, rows, count, top, bound, lean):
    ranking = jax.random.permutation(stream_key, count)
    heavy_load, ordinary = portions_of(count, rows * top, bound, lean, True), portions_of(count, rows * top, bound, lean, False)
    places = jnp.arange(count)

    def named(sizes, rotation):
        used = int((sizes > 0).sum())
        fixed = max(1, used // 4)
        shifted = fixed + (places - fixed + rotation * (used - fixed)) % max(1, count - fixed)
        return jnp.zeros((count,), jnp.int32).at[ranking[jnp.where(places < fixed, places, shifted)]].set(jnp.asarray(sizes, jnp.int32))

    sizes = jnp.where(number % 4 == 0, named(heavy_load, number // 4), named(ordinary, number - number // 4 - 1))
    mixed = jax.random.permutation(jax.random.fold_in(own, 3), count)
    donor, taker = mixed[0:count // 2 * 2:2], mixed[1:count // 2 * 2:2]
    margin = jnp.minimum(sizes[donor] - 1, bound - sizes[taker]) // 2
    margin = jnp.where((donor == ranking[0]) | (taker == ranking[0]) | (sizes[taker] == 0), 0, jnp.maximum(margin, 0))
    shifted = jax.random.randint(jax.random.fold_in(own, 4), (count // 2,), 0, 1 << 20) % (margin + 1)
    sizes = sizes.at[donor].add(-shifted).at[taker].add(shifted)
    members = jnp.searchsorted(jnp.cumsum(sizes), jnp.arange(rows * top), side="right").astype(jnp.int32)
    grid = members.reshape(top, rows).T
    grid = grid[jax.random.permutation(jax.random.fold_in(own, 1), rows)]
    rotation = jax.random.randint(jax.random.fold_in(own, 2), (rows, 1), 0, top)
    return jnp.take_along_axis(grid, (jnp.arange(top)[None, :] + rotation) % top, axis=1)


def portions_of(number_of, total, most, lean, full):
    weights = [(1 << 20) // math.isqrt(rank ** lean) + 1 for rank in range(1, number_of + 1)]
    largest = most if full else min(most, max(-(-total // number_of), total * weights[0] // sum(weights)))
    least = 1 if total - largest >= number_of - 1 else 0
    counts, surplus = [largest] + [least] * (number_of - 1), total - largest - least * (number_of - 1)
    while surplus > 0:
        free = [i for i in range(1, number_of) if counts[i] < largest] or [i for i in range(1, number_of) if counts[i] < most]
        pool, left = sum([weights[i] for i in free]), surplus
        for i in free:
            extra = min(most - counts[i], max(1, left * weights[i] // pool), surplus)
            counts[i] = counts[i] + extra
            surplus = surplus - extra
    return np.array(counts)


def setup_inputs(seed: int = 0) -> dict:
    streams_of = jax.random.split(jax.random.key(seed), 9)
    tail_q = draw_tail_q(jax.random.fold_in(streams_of[8], 71), 0)
    prompt_kv = draw_prompt_kv(jax.random.fold_in(streams_of[8], 71), 0)
    dest_owner_keys = jax.random.split(jax.random.fold_in(streams_of[2], 1), N_GRP * N_CTX * NB // NB)
    dest_owner_turns = jax.random.permutation(jax.random.fold_in(streams_of[2], 3), N_GRP * N_CTX * NB // NB)
    dest_owner = jax.vmap(lambda own, number: shared_out(jax.random.fold_in(streams_of[2], 2), own, number, NB, N_GRP, 1, CAP, 2))(dest_owner_keys, dest_owner_turns).reshape((N_GRP, N_CTX, NB, 1))
    dest_row = set_ends(jax.random.randint(streams_of[3], (N_GRP, N_CTX, NB), 0, ROW_GRP), jax.random.fold_in(streams_of[3], 1), 0, ROW_GRP - 1).astype(jnp.int32)
    dec_q = draw_dec_q(jax.random.fold_in(streams_of[8], 71), 0)
    new_kv = draw_new_kv(jax.random.fold_in(streams_of[8], 71), 0)
    res_kv = draw_res_kv(jax.random.fold_in(streams_of[8], 71), 0)
    lens = uneven(streams_of[7], ROWS, ROWS * RES // 2, RES, 2).astype(jnp.int32)
    return dict(tail_q=tail_q, prompt_kv=prompt_kv, dest_owner=dest_owner, dest_row=dest_row, dec_q=dec_q, new_kv=new_kv, res_kv=res_kv, lens=lens)


def prefill_prompt(operands):
    queries, prompt = operands
    index = jnp.arange(PROMPT)
    offset = index % SEQ_DEV
    tail_pos = jnp.where(offset >= PRE_DEV, index // SEQ_DEV * TAIL_DEV + offset - PRE_DEV, -1)
    allowed = tail_pos[None, :] <= jnp.arange(TAIL)[:, None]
    heads_q = queries.reshape(TAIL, KVH, GROUP, HD).transpose(1, 0, 2, 3)
    heads_k = prompt[:, :KVD].reshape(PROMPT, KVH, HD).transpose(1, 0, 2)
    heads_v = prompt[:, KVD:].reshape(PROMPT, KVH, HD).transpose(1, 0, 2)
    scale = 1.0 / math.sqrt(HD)

    def one_head(parts):
        query, keys, values = parts
        scores = jnp.einsum('cgd,pd->cgp', query.astype(jnp.float32), keys.astype(jnp.float32)) * scale
        scores = jnp.where(allowed[:, None, :], scores, -jnp.inf)
        peak = lax.optimization_barrier(jnp.max(scores, axis=-1, keepdims=True))
        weights = jnp.exp(scores - peak)
        total = lax.optimization_barrier(jnp.sum(weights, axis=-1))
        mixed = jnp.einsum('cgp,pd->cgd', weights, values.astype(jnp.float32))
        return mixed / total[..., None]
    result = lax.map(one_head, (heads_q, heads_k, heads_v))
    return result.transpose(1, 0, 2, 3).reshape(TAIL, QD).astype(jnp.bfloat16)

def reference(tail_q, prompt_kv, dest_owner, dest_row, dec_q, new_kv, res_kv, lens):
    prefill_out = lax.map(prefill_prompt, (tail_q, prompt_kv))
    scale = 1.0 / math.sqrt(HD)
    target = (dest_owner[..., 0] * ROW_GRP + dest_row).reshape(-1).astype(jnp.int32)
    blocks = prompt_kv.reshape(N_GRP * N_CTX * NB, BLK, 2 * KVD)
    block_k = blocks[:, :, :KVD].reshape(-1, BLK, KVH, HD).transpose(2, 0, 1, 3)
    block_v = blocks[:, :, KVD:].reshape(-1, BLK, KVH, HD).transpose(2, 0, 1, 3)
    res_k = res_kv[:, :, :KVD].reshape(ROWS, RES, KVH, HD).transpose(2, 0, 1, 3)
    res_v = res_kv[:, :, KVD:].reshape(ROWS, RES, KVH, HD).transpose(2, 0, 1, 3)
    new_k = new_kv[:, :, :KVD].reshape(ROWS, 2, KVH, HD).transpose(2, 0, 1, 3)
    new_v = new_kv[:, :, KVD:].reshape(ROWS, 2, KVH, HD).transpose(2, 0, 1, 3)
    heads_q = dec_q.reshape(ROWS, 2, KVH, GROUP, HD).transpose(2, 0, 1, 3, 4)
    live = jnp.arange(RES)[None, :] < lens[:, None]
    causal = jnp.arange(2)[None, :] <= jnp.arange(2)[:, None]

    def one_head(parts):
        query, key_new, value_new, key_res, value_res, key_blk, value_blk = parts
        query = query.astype(jnp.float32)
        score_res = jnp.einsum('rtgd,rpd->rtgp', query, key_res.astype(jnp.float32)) * scale
        score_res = jnp.where(live[:, None, None, :], score_res, -jnp.inf)
        score_new = jnp.einsum('rtgd,rud->rtgu', query, key_new.astype(jnp.float32)) * scale
        score_new = jnp.where(causal[None, :, None, :], score_new, -jnp.inf)
        query_blk = query[target]
        score_blk = jnp.einsum('ntgd,nbd->ntgb', query_blk, key_blk.astype(jnp.float32)) * scale
        blk_peak = jax.ops.segment_max(lax.optimization_barrier(jnp.max(score_blk, axis=-1)), target, num_segments=ROWS)
        peak = jnp.maximum(jnp.maximum(lax.optimization_barrier(jnp.max(score_res, axis=-1)), lax.optimization_barrier(jnp.max(score_new, axis=-1))), blk_peak)
        weight_res = jnp.exp(score_res - peak[..., None])
        weight_new = jnp.exp(score_new - peak[..., None])
        weight_blk = jnp.exp(score_blk - peak[target][..., None])
        total = lax.optimization_barrier(jnp.sum(weight_res, axis=-1)) + lax.optimization_barrier(jnp.sum(weight_new, axis=-1))
        total = total + jax.ops.segment_sum(lax.optimization_barrier(jnp.sum(weight_blk, axis=-1)), target, num_segments=ROWS)
        mixed = jnp.einsum('rtgp,rpd->rtgd', weight_res, value_res.astype(jnp.float32))
        mixed = mixed + jnp.einsum('rtgu,rud->rtgd', weight_new, value_new.astype(jnp.float32))
        blk_mixed = jnp.einsum('ntgb,nbd->ntgd', weight_blk, value_blk.astype(jnp.float32))
        mixed = mixed + jax.ops.segment_sum(blk_mixed, target, num_segments=ROWS)
        return mixed / total[..., None]
    result = lax.map(one_head, (heads_q, new_k, new_v, res_k, res_v, block_k, block_v))
    decode_out = result.transpose(1, 2, 0, 3, 4).reshape(ROWS, 2, QD).astype(jnp.bfloat16)
    return (prefill_out, decode_out)
```

```python
import functools
import math

import jax
import jax.numpy as jnp
from jax import lax
from jax.experimental import pallas as pl
from jax.experimental.pallas import tpu as pltpu
from jax.sharding import PartitionSpec as P

HD = 128
KVH = 8
GROUP = 8
PRE_DEV = 496
TAIL_DEV = 64
BLK = 16
ROW_GRP = 4
RES_DEV = 128
KVD = 1024
SEQ_DEV = 560
N_CTX = 8
N_GRP = 16

KEYS = N_CTX * SEQ_DEV
TAIL = N_CTX * TAIL_DEV
SEND_ROWS = SEQ_DEV + 16
FLAT = N_CTX * SEND_ROWS
Q_ROWS = GROUP * TAIL_DEV
VECS = 2 * GROUP
OWN_VECS = ROW_GRP * VECS
PART_ROWS = OWN_VECS + 16
QPART_ROWS = Q_ROWS + PART_ROWS

FLOOR = -1e30
LOG2E = 1.4426950408889634
COEF = LOG2E / math.sqrt(HD)
VMEM = 56 * 2**20
NT = (((1,), (1,)), ((), ()))


def widen_query(q):
    scaled = q.astype(jnp.float32) * COEF
    high = scaled.astype(jnp.bfloat16)
    low = (scaled - high.astype(jnp.float32)).astype(jnp.bfloat16)
    return jnp.concatenate([high, low], axis=1)


def part_of(acc, peak):
    rows = acc.shape[0]
    total = jnp.maximum(acc[:, HD:], 1.0)
    out = (acc[:, :HD] / total).astype(jnp.bfloat16)
    weight = peak + jnp.log2(total)
    diag = lax.broadcasted_iota(jnp.int32, (rows, HD), 0) == lax.broadcasted_iota(
        jnp.int32, (rows, HD), 1
    )
    line = jnp.sum(jnp.where(diag, weight, 0.0), axis=0, keepdims=True)
    first = line.astype(jnp.bfloat16)
    rest = line - first.astype(jnp.float32)
    second = rest.astype(jnp.bfloat16)
    third = rest - second.astype(jnp.float32)
    place = lax.broadcasted_iota(jnp.int32, (16, HD), 0)
    stats = jnp.where(
        place == 0,
        first.astype(jnp.float32),
        jnp.where(place == 1, second.astype(jnp.float32), jnp.where(place == 2, third, 0.0)),
    )
    return out, stats.astype(jnp.bfloat16)


def pack_kv_kernel(k_ref, v_ref, label_ref, out_ref):
    out_ref[0, :SEQ_DEV, :HD] = k_ref[...]
    out_ref[0, :SEQ_DEV, HD:] = v_ref[...]
    out_ref[0, SEQ_DEV:, :] = label_ref[...]


def pack_kv(kv, labels):
    return pl.pallas_call(
        pack_kv_kernel,
        grid=(KVH,),
        in_specs=[
            pl.BlockSpec((SEQ_DEV, HD), lambda e: (0, e)),
            pl.BlockSpec((SEQ_DEV, HD), lambda e: (0, KVH + e)),
            pl.BlockSpec((16, 2 * HD), lambda e: (0, 0)),
        ],
        out_specs=pl.BlockSpec((1, SEND_ROWS, 2 * HD), lambda e: (e, 0, 0)),
        out_shape=jax.ShapeDtypeStruct((KVH, SEND_ROWS, 2 * HD), jnp.bfloat16),
        cost_estimate=pl.CostEstimate(flops=0, bytes_accessed=4600000, transcendentals=0),
        name="pack_kv",
    )(kv, kv, labels)


def query_res_kernel(live_ref, q_ref, dq_ref, k_ref, v_ref, out_ref, vs_ref):
    for head in range(GROUP):
        out_ref[0, head * TAIL_DEV : (head + 1) * TAIL_DEV, :] = q_ref[
            :, head * HD : (head + 1) * HD
        ]
    keys = k_ref[...].reshape(ROW_GRP * RES_DEV, HD)
    vs_ref[:, :HD] = v_ref[...].reshape(ROW_GRP * RES_DEV, HD)
    vs_ref[:, HD:] = jnp.ones((ROW_GRP * RES_DEV, HD), jnp.bfloat16)
    query = widen_query(dq_ref[0])
    scores = lax.dot_general(query[:, :HD], keys, NT, preferred_element_type=jnp.float32)
    scores += lax.dot_general(query[:, HD:], keys, NT, preferred_element_type=jnp.float32)
    shape = (OWN_VECS, ROW_GRP * RES_DEV)
    row = lax.broadcasted_iota(jnp.int32, shape, 0)
    col = lax.broadcasted_iota(jnp.int32, shape, 1)
    for r in range(ROW_GRP):
        inside = (row >= r * VECS) & (row < (r + 1) * VECS)
        low, high = r * RES_DEV, jnp.clip(live_ref[r], 0, RES_DEV) + r * RES_DEV
        scores = jnp.where(inside & ((col < low) | (col >= high)), -jnp.inf, scores)
    peak = jnp.maximum(jnp.max(scores, axis=1, keepdims=True), FLOOR)
    weights = jnp.exp2(scores - peak).astype(jnp.bfloat16)
    acc = jnp.dot(weights, vs_ref[...], preferred_element_type=jnp.float32)
    out, stats = part_of(acc, peak)
    out_ref[0, Q_ROWS : Q_ROWS + OWN_VECS, :] = out
    out_ref[0, Q_ROWS + OWN_VECS :, :] = stats


def query_res(live, tail_q, dec_vecs, res_kv):
    return pl.pallas_call(
        query_res_kernel,
        grid=(KVH,),
        in_specs=[
            pl.BlockSpec(memory_space=pltpu.SMEM),
            pl.BlockSpec((TAIL_DEV, GROUP * HD), lambda e: (0, e)),
            pl.BlockSpec((1, OWN_VECS, HD), lambda e: (e, 0, 0)),
            pl.BlockSpec((ROW_GRP, RES_DEV, HD), lambda e: (0, 0, e)),
            pl.BlockSpec((ROW_GRP, RES_DEV, HD), lambda e: (0, 0, KVH + e)),
        ],
        out_specs=pl.BlockSpec((1, QPART_ROWS, HD), lambda e: (e, 0, 0)),
        out_shape=jax.ShapeDtypeStruct((KVH, QPART_ROWS, HD), jnp.bfloat16),
        scratch_shapes=[pltpu.VMEM((ROW_GRP * RES_DEV, 2 * HD), jnp.bfloat16)],
        cost_estimate=pl.CostEstimate(flops=500000000, bytes_accessed=4600000, transcendentals=0),
        name="query_res",
    )(live, tail_q, dec_vecs, res_kv, res_kv)


def prefill_kernel(chunks, q_ref, kv_ref, o_ref, k_s, v_s):
    shard = pl.program_id(0)

    @pl.when(shard == 0)
    def _():
        for s in range(N_CTX):
            for dst, src, n in (
                (s * TAIL_DEV, PRE_DEV, TAIL_DEV),
                (TAIL + s * PRE_DEV, 0, PRE_DEV),
            ):
                keys = kv_ref[s, src : src + n, :HD]
                k_s[dst : dst + n, :HD] = keys
                k_s[dst : dst + n, HD:] = keys
                v_s[dst : dst + n, :HD] = kv_ref[s, src : src + n, HD:]
        v_s[:, HD:] = jnp.ones((KEYS, HD), jnp.bfloat16)

    query = widen_query(q_ref[0])
    peak = acc = None
    start = 0
    for n in chunks:
        scores = lax.dot_general(
            query, k_s[start : start + n, :], NT, preferred_element_type=jnp.float32
        )
        if start < TAIL:
            token = (
                lax.broadcasted_iota(jnp.int32, (Q_ROWS, n), 0) % TAIL_DEV + shard * TAIL_DEV
            )
            col = lax.broadcasted_iota(jnp.int32, (Q_ROWS, n), 1) + start
            scores = jnp.where((col > token) & (col < TAIL), -jnp.inf, scores)
        top = jnp.max(scores, axis=1, keepdims=True)
        new_peak = top if peak is None else jnp.maximum(peak, top)
        weights = jnp.exp2(scores - new_peak).astype(jnp.bfloat16)
        mixed = jnp.dot(weights, v_s[start : start + n, :], preferred_element_type=jnp.float32)
        acc = mixed if peak is None else acc * jnp.exp2(peak - new_peak) + mixed
        peak = new_peak
        start += n
    out = (acc[:, :HD] / acc[:, HD:]).astype(jnp.bfloat16)
    for head in range(GROUP):
        o_ref[0, :, head * HD : (head + 1) * HD] = out[head * TAIL_DEV : (head + 1) * TAIL_DEV]


def prefill(queries, kv):
    return pl.pallas_call(
        functools.partial(prefill_kernel, (1024, 1024, 1024, 1408)),
        grid=(N_CTX,),
        in_specs=[
            pl.BlockSpec((1, Q_ROWS, HD), lambda d: (d, 0, 0)),
            pl.BlockSpec((N_CTX, SEND_ROWS, 2 * HD), lambda d: (0, 0, 0)),
        ],
        out_specs=pl.BlockSpec((1, TAIL_DEV, GROUP * HD), lambda d: (d, 0, 0)),
        out_shape=jax.ShapeDtypeStruct((N_CTX, TAIL_DEV, GROUP * HD), jnp.bfloat16),
        scratch_shapes=[
            pltpu.VMEM((KEYS, 2 * HD), jnp.bfloat16),
            pltpu.VMEM((KEYS, 2 * HD), jnp.bfloat16),
        ],
        compiler_params=pltpu.CompilerParams(vmem_limit_bytes=VMEM),
        cost_estimate=pl.CostEstimate(
            flops=30000000000, bytes_accessed=5000000, transcendentals=18000000
        ),
        name="prefill",
    )(queries, kv)


BLK_ROWS = 512
BLK_CHUNK = 1536


def blocks_kernel(q_ref, kv_ref, label_ref, o_ref, k_s, v_s):
    part = pl.program_id(0)

    @pl.when(part == 0)
    def _():
        keys = kv_ref[:, :HD]
        k_s[:, :HD] = keys
        k_s[:, HD:] = keys
        v_s[:, :HD] = kv_ref[:, HD:]
        v_s[:, HD:] = jnp.ones((FLAT, HD), jnp.bfloat16)

    query = widen_query(q_ref[...])
    peak = acc = None
    row = lax.broadcasted_iota(jnp.int32, (BLK_ROWS, BLK_CHUNK), 0) + part * BLK_ROWS
    row = row // VECS
    for start in range(0, FLAT, BLK_CHUNK):
        end = start + BLK_CHUNK
        scores = lax.dot_general(query, k_s[start:end, :], NT, preferred_element_type=jnp.float32)
        scores = jnp.where(label_ref[:, start:end] == row, scores, -jnp.inf)
        top = jnp.maximum(jnp.max(scores, axis=1, keepdims=True), FLOOR)
        new_peak = top if peak is None else jnp.maximum(peak, top)
        weights = jnp.exp2(scores - new_peak).astype(jnp.bfloat16)
        mixed = jnp.dot(weights, v_s[start:end, :], preferred_element_type=jnp.float32)
        acc = mixed if peak is None else acc * jnp.exp2(peak - new_peak) + mixed
        peak = new_peak
    for i in range(BLK_ROWS // OWN_VECS):
        span = slice(i * OWN_VECS, (i + 1) * OWN_VECS)
        out, stats = part_of(acc[span], peak[span])
        o_ref[i, :OWN_VECS, :] = out
        o_ref[i, OWN_VECS:, :] = stats


def blocks(queries, kv, labels):
    rows = queries.shape[0]
    return pl.pallas_call(
        blocks_kernel,
        grid=(rows // BLK_ROWS,),
        in_specs=[
            pl.BlockSpec((BLK_ROWS, HD), lambda i: (i, 0)),
            pl.BlockSpec((FLAT, 2 * HD), lambda i: (0, 0)),
            pl.BlockSpec((1, FLAT), lambda i: (0, 0)),
        ],
        out_specs=pl.BlockSpec((BLK_ROWS // OWN_VECS, PART_ROWS, HD), lambda i: (i, 0, 0)),
        out_shape=jax.ShapeDtypeStruct((rows // OWN_VECS, PART_ROWS, HD), jnp.bfloat16),
        scratch_shapes=[
            pltpu.VMEM((FLAT, 2 * HD), jnp.bfloat16),
            pltpu.VMEM((FLAT, 2 * HD), jnp.bfloat16),
        ],
        compiler_params=pltpu.CompilerParams(vmem_limit_bytes=VMEM),
        cost_estimate=pl.CostEstimate(
            flops=8000000000, bytes_accessed=3000000, transcendentals=4700000
        ),
        name="blocks",
    )(queries, kv, labels)


def finish_kernel(blk_ref, res_ref, q_ref, nk_ref, nv_ref, o_ref):
    shape = (OWN_VECS, HD)
    row = lax.broadcasted_iota(jnp.int32, shape, 0)
    col = lax.broadcasted_iota(jnp.int32, shape, 1)
    diag = row == col
    query = widen_query(q_ref[...])
    keys = jnp.concatenate([nk_ref[...], jnp.zeros((HD - 16, HD), jnp.bfloat16)], axis=0)
    values = jnp.concatenate([nv_ref[...], jnp.zeros((HD - 16, HD), jnp.bfloat16)], axis=0)
    scores = lax.dot_general(query[:, :HD], keys, NT, preferred_element_type=jnp.float32)
    scores += lax.dot_general(query[:, HD:], keys, NT, preferred_element_type=jnp.float32)
    open_ = (col // 2 == row // VECS) & (col % 2 <= row % VECS // GROUP)
    scores = jnp.where(open_, scores, -jnp.inf)
    outs, weights = [], []
    for ref, count, base in ((blk_ref, N_GRP, 0), (res_ref, N_CTX, 0)):
        for i in range(count):
            outs.append(ref[i, base : base + OWN_VECS, :])
            stats = ref[i, base + OWN_VECS : base + PART_ROWS, :].astype(jnp.float32)
            line = jnp.sum(stats[0:8], axis=0, keepdims=True)
            weights.append(jnp.sum(jnp.where(diag, line, 0.0), axis=1, keepdims=True))
    peak = jnp.max(scores, axis=1, keepdims=True)
    for weight in weights:
        peak = jnp.maximum(peak, weight)
    new = jnp.exp2(scores - peak)
    total = jnp.sum(new, axis=1, keepdims=True)
    mixed = jnp.dot(new.astype(jnp.bfloat16), values, preferred_element_type=jnp.float32)
    for out, weight in zip(outs, weights):
        share = jnp.exp2(weight - peak)
        total += share
        mixed += share * out.astype(jnp.float32)
    o_ref[...] = (mixed / total).astype(jnp.bfloat16)


def finish(block_parts, res_parts, queries, new_keys, new_values):
    return pl.pallas_call(
        finish_kernel,
        out_shape=jax.ShapeDtypeStruct((OWN_VECS, HD), jnp.bfloat16),
        cost_estimate=pl.CostEstimate(flops=5000000, bytes_accessed=600000, transcendentals=0),
        name="finish",
    )(block_parts, res_parts, queries, new_keys, new_values)


def place_kernel(in_ref, out_ref):
    out_ref[...] = in_ref[0]


def place(parts):
    return pl.pallas_call(
        place_kernel,
        grid=(KVH,),
        in_specs=[pl.BlockSpec((1, TAIL_DEV, GROUP * HD), lambda e: (e, 0, 0))],
        out_specs=pl.BlockSpec((TAIL_DEV, GROUP * HD), lambda e: (0, e)),
        out_shape=jax.ShapeDtypeStruct((TAIL_DEV, KVH * GROUP * HD), jnp.bfloat16),
        cost_estimate=pl.CostEstimate(flops=0, bytes_accessed=2100000, transcendentals=0),
        name="place",
    )(parts)


def local(tail_q, prompt_kv, dest_owner, dest_row, dec_q, new_kv, res_kv, lens):
    ctx = lax.axis_index("ctx")
    block_row = dest_owner.reshape(-1) * ROW_GRP + dest_row.reshape(-1)
    labels = jnp.pad(jnp.repeat(block_row, BLK), (0, 16), constant_values=-1)
    labels = jnp.pad(labels, (0, 16 * 2 * HD - SEND_ROWS)).reshape(16, 2 * HD)
    sent_kv = pack_kv(prompt_kv[0], labels.astype(jnp.bfloat16))
    got_kv = lax.all_to_all(sent_kv, "ctx", split_axis=0, concat_axis=0, tiled=True)

    dec_vecs = dec_q.reshape(ROW_GRP * 2, KVH, GROUP, HD).transpose(1, 0, 2, 3)
    dec_vecs = dec_vecs.reshape(KVH, OWN_VECS, HD)
    own_vecs = lax.dynamic_index_in_dim(dec_vecs, ctx, 0, keepdims=False)
    spread = jnp.broadcast_to(own_vecs[None], (N_GRP, OWN_VECS, HD))
    all_vecs = lax.all_to_all(spread, "grp", split_axis=0, concat_axis=0, tiled=True)

    sent_q = query_res(lens - ctx * RES_DEV, tail_q[0], dec_vecs, res_kv)
    got_q = lax.all_to_all(sent_q, "ctx", split_axis=0, concat_axis=0, tiled=True)

    got_labels = got_kv[:, SEQ_DEV:, :].reshape(N_CTX, -1)[:, :SEND_ROWS]
    got_labels = got_labels.reshape(1, FLAT).astype(jnp.int32)
    block_parts = blocks(
        all_vecs.reshape(-1, HD), got_kv.reshape(FLAT, 2 * HD), got_labels
    )
    block_parts = lax.all_to_all(block_parts, "grp", split_axis=0, concat_axis=0, tiled=True)

    prefill_parts = prefill(got_q, got_kv)
    prefill_parts = lax.all_to_all(
        prefill_parts, "ctx", split_axis=0, concat_axis=0, tiled=True
    )

    own_new = new_kv.reshape(ROW_GRP * 2, 2, KVH, HD)
    own_new = lax.dynamic_index_in_dim(own_new, ctx, 2, keepdims=False)
    own_new = jnp.pad(own_new, ((0, 8), (0, 0), (0, 0)))
    decode = finish(
        block_parts, got_q[:, Q_ROWS:, :], own_vecs, own_new[:, 0], own_new[:, 1]
    )
    decode_out = decode.reshape(ROW_GRP, 2, GROUP * HD)
    prefill_out = place(prefill_parts)[None]
    return prefill_out, decode_out


def solution(mesh):
    return jax.shard_map(
        local,
        mesh=mesh,
        in_specs=(
            P("grp", "ctx", None),
            P("grp", "ctx", None),
            P("grp", "ctx", None, None),
            P("grp", "ctx", None),
            P("grp", None, None),
            P("grp", None, None),
            P("grp", "ctx", None),
            P("grp"),
        ),
        out_specs=(P("grp", "ctx", None), P("grp", None, "ctx")),
        check_vma=False,
    )
```

```python
import functools
import math

import jax
import jax.numpy as jnp
from jax import lax
from jax.experimental import pallas as pl
from jax.experimental.pallas import tpu as pltpu
from jax.sharding import PartitionSpec as P

HD = 128
KVH = 8
GROUP = 8
PRE_DEV = 496
TAIL_DEV = 64
BLK = 16
ROW_GRP = 4
RES_DEV = 128
KVD = 1024
SEQ_DEV = 560
N_CTX = 8
N_GRP = 16

KEYS = N_CTX * SEQ_DEV
TAIL = N_CTX * TAIL_DEV
Q_ROWS = GROUP * TAIL_DEV
SEND_ROWS = SEQ_DEV + 16
VECS = 2 * GROUP
OWN_VECS = ROW_GRP * VECS
PART_ROWS = OWN_VECS + 16
QPART_ROWS = Q_ROWS + PART_ROWS
STEP = 2
ROWS_STEP = STEP * Q_ROWS
SPAN = 512
REST = SEQ_DEV - SPAN
BITS = (1, 4, 8, 2)

FLOOR = -1e30
LOG2E = 1.4426950408889634
COEF = LOG2E / math.sqrt(HD)
VMEM = 58 * 2**20
NT = (((1,), (1,)), ((), ()))


def widen_query(q):
    scaled = q.astype(jnp.float32) * COEF
    high = scaled.astype(jnp.bfloat16)
    low = (scaled - high.astype(jnp.float32)).astype(jnp.bfloat16)
    return jnp.concatenate([high, low], axis=1)


def part_of(acc, peak):
    rows = acc.shape[0]
    total = jnp.maximum(acc[:, HD:], 1.0)
    out = (acc[:, :HD] / total).astype(jnp.bfloat16)
    weight = peak + jnp.log2(total)
    diag = lax.broadcasted_iota(jnp.int32, (rows, HD), 0) == lax.broadcasted_iota(
        jnp.int32, (rows, HD), 1
    )
    line = jnp.sum(jnp.where(diag, weight, 0.0), axis=0, keepdims=True)
    first = line.astype(jnp.bfloat16)
    rest = line - first.astype(jnp.float32)
    second = rest.astype(jnp.bfloat16)
    third = rest - second.astype(jnp.float32)
    place = lax.broadcasted_iota(jnp.int32, (16, HD), 0)
    stats = jnp.where(
        place == 0,
        first.astype(jnp.float32),
        jnp.where(place == 1, second.astype(jnp.float32), jnp.where(place == 2, third, 0.0)),
    )
    return out, stats.astype(jnp.bfloat16)


def spans(total):
    return [(at, min(SPAN, total - at)) for at in range(0, total, SPAN)]


def whole(space=pltpu.VMEM):
    return pl.BlockSpec(memory_space=space)


def pack_kernel(owner_hbm, row_hbm, kv_ref, out_ref, owner_ref, row_ref, sems, small):
    named = [
        pltpu.make_async_copy(owner_hbm, owner_ref, small.at[0]),
        pltpu.make_async_copy(row_hbm, row_ref, small.at[1]),
    ]
    for copy in named:
        copy.start()
    copies = []

    def add(src, dst):
        copies.append(pltpu.make_async_copy(src, dst, sems.at[len(copies)]))
        copies[-1].start()

    for e in range(KVH):
        for half in range(2):
            lanes = pl.ds(half * HD, HD)
            add(
                kv_ref.at[:, pl.ds(half * KVD + e * HD, HD)],
                out_ref.at[e, pl.ds(0, SEQ_DEV), lanes],
            )
    for copy in named:
        copy.wait()
    shape = (16, 2 * HD)
    place = lax.broadcasted_iota(jnp.int32, shape, 0) * (2 * HD)
    place += lax.broadcasted_iota(jnp.int32, shape, 1)
    rest = place - SPAN - lax.axis_index("ctx") * REST
    rest = jnp.where((rest >= 0) & (rest < REST), rest + SPAN, SEQ_DEV)
    block = jnp.where(place < SPAN, place, rest) // BLK
    labels = jnp.zeros(shape, jnp.float32)
    for b in range(SEQ_DEV // BLK):
        value = (owner_ref[b] * ROW_GRP + row_ref[b]).astype(jnp.float32)
        labels = jnp.where(block == b, value, labels)
    labels = labels.astype(jnp.bfloat16)
    for e in range(KVH):
        out_ref[e, SEQ_DEV:, :] = labels
    for copy in copies:
        copy.wait()


def pack(owner, row, kv):
    return pl.pallas_call(
        pack_kernel,
        in_specs=[whole(pltpu.HBM)] * 3,
        out_specs=whole(),
        out_shape=jax.ShapeDtypeStruct((KVH, SEND_ROWS, 2 * HD), jnp.bfloat16),
        scratch_shapes=[
            pltpu.SMEM((SEQ_DEV // BLK,), jnp.int32),
            pltpu.SMEM((SEQ_DEV // BLK,), jnp.int32),
            pltpu.SemaphoreType.DMA((KVH * 2,)),
            pltpu.SemaphoreType.DMA((2,)),
        ],
        compiler_params=pltpu.CompilerParams(vmem_limit_bytes=VMEM),
        cost_estimate=pl.CostEstimate(flops=0, bytes_accessed=4600000, transcendentals=0),
        name="pack",
    )(owner, row, kv)


def query_res_kernel(live_ref, q_ref, dq_ref, k_ref, v_ref, out_ref, vs_ref):
    for head in range(GROUP):
        out_ref[0, head * TAIL_DEV : (head + 1) * TAIL_DEV, :] = q_ref[
            :, head * HD : (head + 1) * HD
        ]
    keys = k_ref[...].reshape(ROW_GRP * RES_DEV, HD)
    vs_ref[:, :HD] = v_ref[...].reshape(ROW_GRP * RES_DEV, HD)
    vs_ref[:, HD:] = jnp.ones((ROW_GRP * RES_DEV, HD), jnp.bfloat16)
    query = widen_query(dq_ref[0])
    scores = lax.dot_general(query[:, :HD], keys, NT, preferred_element_type=jnp.float32)
    scores += lax.dot_general(query[:, HD:], keys, NT, preferred_element_type=jnp.float32)
    shape = (OWN_VECS, ROW_GRP * RES_DEV)
    row = lax.broadcasted_iota(jnp.int32, shape, 0)
    col = lax.broadcasted_iota(jnp.int32, shape, 1)
    for r in range(ROW_GRP):
        inside = (row >= r * VECS) & (row < (r + 1) * VECS)
        low, high = r * RES_DEV, jnp.clip(live_ref[r], 0, RES_DEV) + r * RES_DEV
        scores = jnp.where(inside & ((col < low) | (col >= high)), -jnp.inf, scores)
    peak = jnp.maximum(jnp.max(scores, axis=1, keepdims=True), FLOOR)
    weights = jnp.exp2(scores - peak).astype(jnp.bfloat16)
    acc = jnp.dot(weights, vs_ref[...], preferred_element_type=jnp.float32)
    out, stats = part_of(acc, peak)
    out_ref[0, Q_ROWS : Q_ROWS + OWN_VECS, :] = out
    out_ref[0, Q_ROWS + OWN_VECS :, :] = stats


def query_res(live, tail_q, dec_vecs, res_kv):
    return pl.pallas_call(
        query_res_kernel,
        grid=(KVH,),
        in_specs=[
            pl.BlockSpec(memory_space=pltpu.SMEM),
            pl.BlockSpec((TAIL_DEV, GROUP * HD), lambda e: (0, e)),
            pl.BlockSpec((1, OWN_VECS, HD), lambda e: (e, 0, 0)),
            pl.BlockSpec((ROW_GRP, RES_DEV, HD), lambda e: (0, 0, e)),
            pl.BlockSpec((ROW_GRP, RES_DEV, HD), lambda e: (0, 0, KVH + e)),
        ],
        out_specs=pl.BlockSpec((1, QPART_ROWS, HD), lambda e: (e, 0, 0)),
        out_shape=jax.ShapeDtypeStruct((KVH, QPART_ROWS, HD), jnp.bfloat16),
        scratch_shapes=[pltpu.VMEM((ROW_GRP * RES_DEV, 2 * HD), jnp.bfloat16)],
        cost_estimate=pl.CostEstimate(flops=500000000, bytes_accessed=4600000, transcendentals=0),
        name="query_res",
    )(live, tail_q, dec_vecs, res_kv, res_kv)


def attend(query, k_s, v_s, pieces, masker, ready=None):
    def score(at, n):
        if ready is not None:
            ready(at)
        scores = lax.dot_general(
            query, k_s[at : at + n, :], NT, preferred_element_type=jnp.float32
        )
        return masker(scores, at)

    peak = acc = None
    scores = score(*pieces[0])
    for i, (at, n) in enumerate(pieces):
        later = score(*pieces[i + 1]) if i + 1 < len(pieces) else None
        top = jnp.maximum(jnp.max(scores, axis=1, keepdims=True), FLOOR)
        new_peak = top if peak is None else jnp.maximum(peak, top)
        weights = jnp.exp2(scores - new_peak).astype(jnp.bfloat16)
        mixed = jnp.dot(weights, v_s[at : at + n, :], preferred_element_type=jnp.float32)
        acc = mixed if peak is None else acc * jnp.exp2(peak - new_peak) + mixed
        peak, scores = new_peak, later
    return peak, acc


def fetch(got_ref, got_s, sems):
    copies = [
        pltpu.make_async_copy(got_ref.at[s], got_s.at[s], sems.at[s]) for s in range(N_CTX)
    ]
    for copy in copies:
        copy.start()
    return copies


def fill(k_s, v_s, at, got_s, shard, src, n):
    keys = got_s[shard, src : src + n, :HD]
    k_s[at : at + n, :HD] = keys
    k_s[at : at + n, HD:] = keys
    v_s[at : at + n, :HD] = got_s[shard, src : src + n, HD:]


def shard_queries(got_ref, step):
    parts = [got_ref[step * STEP + g, :Q_ROWS, :] for g in range(STEP)]
    return widen_query(jnp.concatenate(parts, axis=0))


def blocks_kernel(got_ref, dq_ref, o_ref, k_s, v_s, got_s, sems):
    copies = fetch(got_ref, got_s, sems)
    v_s[:, HD:] = jnp.ones((KEYS, HD), jnp.bfloat16)

    def ready(at):
        first = at // SPAN
        if first < N_CTX:
            copies[first].wait()
            fill(k_s, v_s, at, got_s, first, 0, SPAN)
        else:
            for s in range(N_CTX):
                fill(k_s, v_s, at + s * REST, got_s, s, SPAN, REST)

    rows = dq_ref.shape[0]
    row = lax.broadcasted_iota(jnp.int32, (rows, 1), 0)
    place = row // OWN_VECS
    owner = jnp.zeros_like(place)
    for i, bit in enumerate(BITS):
        owner += (place // 2**i % 2) * bit
    row = (owner * ROW_GRP + row % OWN_VECS // VECS).astype(jnp.float32)

    def labels_of(s, first):
        pair = got_s[s, SEQ_DEV:, :].astype(jnp.float32)
        return jnp.concatenate([pair[first : first + 1], pair[first + 1 : first + 2]], axis=1)

    def masker(scores, at):
        if at // SPAN < N_CTX:
            labels = labels_of(at // SPAN, 0)
        else:
            labels = labels_of(0, 2)
            for s in range(1, N_CTX):
                labels += labels_of(s, 2)
            labels = labels[:, : N_CTX * REST]
        return jnp.where(labels == row, scores, -jnp.inf)

    peak, acc = attend(widen_query(dq_ref[...]), k_s, v_s, spans(KEYS), masker, ready)
    for place in range(rows // OWN_VECS):
        owner = sum((place >> i & 1) * bit for i, bit in enumerate(BITS))
        span = slice(place * OWN_VECS, (place + 1) * OWN_VECS)
        out, stats = part_of(acc[span], peak[span])
        o_ref[owner, :OWN_VECS, :] = out
        o_ref[owner, OWN_VECS:, :] = stats


def blocks(got, dec_vecs):
    return pl.pallas_call(
        blocks_kernel,
        in_specs=[whole(pltpu.HBM), whole()],
        out_specs=whole(),
        out_shape=jax.ShapeDtypeStruct((N_GRP, PART_ROWS, HD), jnp.bfloat16),
        scratch_shapes=[
            pltpu.VMEM((KEYS, 2 * HD), jnp.bfloat16),
            pltpu.VMEM((KEYS, 2 * HD), jnp.bfloat16),
            pltpu.VMEM((N_CTX, SEND_ROWS, 2 * HD), jnp.bfloat16),
            pltpu.SemaphoreType.DMA((N_CTX,)),
        ],
        compiler_params=pltpu.CompilerParams(vmem_limit_bytes=VMEM),
        cost_estimate=pl.CostEstimate(
            flops=8000000000, bytes_accessed=3000000, transcendentals=4700000
        ),
        name="blocks",
    )(got, dec_vecs)


def prefill_kernel(got_q_ref, got_ref, o_ref, k_s, v_s, got_s, sems):
    step = pl.program_id(0)

    @pl.when(step == 0)
    def _():
        copies = fetch(got_ref, got_s, sems)
        v_s[:, HD:] = jnp.ones((KEYS, HD), jnp.bfloat16)
        for s in range(N_CTX):
            copies[s].wait()
            fill(k_s, v_s, s * TAIL_DEV, got_s, s, PRE_DEV, TAIL_DEV)
            fill(k_s, v_s, TAIL + s * PRE_DEV, got_s, s, 0, PRE_DEV)

    def masker(scores, at):
        if at >= TAIL:
            return scores
        row = lax.broadcasted_iota(jnp.int32, (ROWS_STEP, 1), 0)
        token = row % TAIL_DEV + (step * STEP + row // Q_ROWS) * TAIL_DEV
        col = lax.broadcasted_iota(jnp.int32, scores.shape, 1) + at
        return jnp.where(col > token, -jnp.inf, scores)

    _, acc = attend(shard_queries(got_q_ref, step), k_s, v_s, spans(KEYS), masker)
    out = (acc[:, :HD] / acc[:, HD:]).astype(jnp.bfloat16)
    for g in range(STEP):
        for head in range(GROUP):
            at = g * Q_ROWS + head * TAIL_DEV
            o_ref[g, :, head * HD : (head + 1) * HD] = out[at : at + TAIL_DEV]


def prefill(got_q, got):
    return pl.pallas_call(
        prefill_kernel,
        grid=(N_CTX // STEP,),
        in_specs=[whole(), whole(pltpu.HBM)],
        out_specs=pl.BlockSpec((STEP, TAIL_DEV, GROUP * HD), lambda i: (i, 0, 0)),
        out_shape=pltpu.HBM((N_CTX, TAIL_DEV, GROUP * HD), jnp.bfloat16),
        scratch_shapes=[
            pltpu.VMEM((KEYS, 2 * HD), jnp.bfloat16),
            pltpu.VMEM((KEYS, 2 * HD), jnp.bfloat16),
            pltpu.VMEM((N_CTX, SEND_ROWS, 2 * HD), jnp.bfloat16),
            pltpu.SemaphoreType.DMA((N_CTX,)),
        ],
        compiler_params=pltpu.CompilerParams(vmem_limit_bytes=VMEM),
        cost_estimate=pl.CostEstimate(
            flops=26000000000, bytes_accessed=6000000, transcendentals=18000000
        ),
        name="prefill",
    )(got_q, got)


def finish_kernel(blk_ref, in_ref, q_ref, nk_ref, nv_ref, o_ref):
    shape = (OWN_VECS, HD)
    row = lax.broadcasted_iota(jnp.int32, shape, 0)
    col = lax.broadcasted_iota(jnp.int32, shape, 1)
    diag = row == col
    query = widen_query(q_ref[...])
    keys = jnp.concatenate([nk_ref[...], jnp.zeros((HD - 16, HD), jnp.bfloat16)], axis=0)
    values = jnp.concatenate([nv_ref[...], jnp.zeros((HD - 16, HD), jnp.bfloat16)], axis=0)
    scores = lax.dot_general(query[:, :HD], keys, NT, preferred_element_type=jnp.float32)
    scores += lax.dot_general(query[:, HD:], keys, NT, preferred_element_type=jnp.float32)
    open_ = (col // 2 == row // VECS) & (col % 2 <= row % VECS // GROUP)
    scores = jnp.where(open_, scores, -jnp.inf)
    outs, weights = [], []
    parts = [(blk_ref[i, :OWN_VECS, :], blk_ref[i, OWN_VECS:, :]) for i in range(N_GRP)]
    for i in range(N_CTX):
        parts.append(
            (in_ref[i, Q_ROWS : Q_ROWS + OWN_VECS, :], in_ref[i, Q_ROWS + OWN_VECS :, :])
        )
    for out, stats in parts:
        outs.append(out)
        line = jnp.sum(stats.astype(jnp.float32)[:8], axis=0, keepdims=True)
        weights.append(jnp.sum(jnp.where(diag, line, 0.0), axis=1, keepdims=True))
    peak = jnp.max(scores, axis=1, keepdims=True)
    for weight in weights:
        peak = jnp.maximum(peak, weight)
    new = jnp.exp2(scores - peak)
    total = jnp.sum(new, axis=1, keepdims=True)
    mixed = jnp.dot(new.astype(jnp.bfloat16), values, preferred_element_type=jnp.float32)
    for out, weight in zip(outs, weights):
        share = jnp.exp2(weight - peak)
        total += share
        mixed += share * out.astype(jnp.float32)
    out = mixed / total
    for token in range(ROW_GRP * 2):
        for head in range(GROUP):
            at = token * GROUP + head
            o_ref[token : token + 1, head * HD : (head + 1) * HD] = out[at : at + 1].astype(
                jnp.bfloat16
            )


def finish(block_parts, got_q, queries, new_keys, new_values):
    return pl.pallas_call(
        finish_kernel,
        in_specs=[whole()] * 5,
        out_specs=whole(),
        out_shape=jax.ShapeDtypeStruct((ROW_GRP * 2, GROUP * HD), jnp.bfloat16),
        compiler_params=pltpu.CompilerParams(vmem_limit_bytes=16 * 2**20),
        cost_estimate=pl.CostEstimate(flops=5000000, bytes_accessed=1600000, transcendentals=0),
        name="finish",
    )(block_parts, got_q, queries, new_keys, new_values)


def place_kernel(in_ref, out_ref, sems):
    copies = []
    for e in range(KVH):
        lanes = pl.ds(e * GROUP * HD, GROUP * HD)
        copies.append(pltpu.make_async_copy(in_ref.at[e], out_ref.at[:, lanes], sems.at[e]))
        copies[-1].start()
    for copy in copies:
        copy.wait()


def place(parts):
    return pl.pallas_call(
        place_kernel,
        in_specs=[whole()],
        out_specs=whole(pl.ANY),
        out_shape=jax.ShapeDtypeStruct((TAIL_DEV, KVH * GROUP * HD), jnp.bfloat16),
        scratch_shapes=[pltpu.SemaphoreType.DMA((KVH,))],
        compiler_params=pltpu.CompilerParams(vmem_limit_bytes=8 * 2**20),
        cost_estimate=pl.CostEstimate(flops=0, bytes_accessed=2100000, transcendentals=0),
        name="place",
    )(parts)


def spread_over(values, axis, size, before, got):
    values = values + before[0, :1, :] * 0
    me = lax.axis_index(axis)
    for bit in BITS:
        if bit == BITS[-1]:
            values = values + got[0, :1, :HD] * 0
        other = lax.ppermute(values, axis, [(i, i ^ bit) for i in range(size)])
        upper = (me & bit) != 0
        values = jnp.concatenate(
            [jnp.where(upper, other, values), jnp.where(upper, values, other)], axis=0
        )
    return values


def local(tail_q, prompt_kv, dest_owner, dest_row, dec_q, new_kv, res_kv, lens):
    ctx = lax.axis_index("ctx")
    sent = pack(dest_owner.reshape(-1), dest_row.reshape(-1), prompt_kv[0])
    got = lax.all_to_all(sent, "ctx", split_axis=0, concat_axis=0, tiled=True)

    dec_vecs = dec_q.reshape(ROW_GRP * 2, KVH, GROUP, HD).transpose(1, 0, 2, 3)
    dec_vecs = dec_vecs.reshape(KVH, OWN_VECS, HD)
    own_vecs = lax.dynamic_index_in_dim(dec_vecs, ctx, 0, keepdims=False)
    sent_q = query_res(lens - ctx * RES_DEV, tail_q[0], dec_vecs, res_kv)
    got_q = lax.all_to_all(sent_q, "ctx", split_axis=0, concat_axis=0, tiled=True)
    all_vecs = spread_over(own_vecs, "grp", N_GRP, sent_q, got)

    block_parts = blocks(got, all_vecs)
    block_parts = lax.all_to_all(block_parts, "grp", split_axis=0, concat_axis=0, tiled=True)
    parts = prefill(got_q, got)
    parts = lax.all_to_all(parts, "ctx", split_axis=0, concat_axis=0, tiled=True)

    own_new = new_kv.reshape(ROW_GRP * 2, 2, KVH, HD)
    own_new = lax.dynamic_index_in_dim(own_new, ctx, 2, keepdims=False)
    own_new = jnp.pad(own_new, ((0, 8), (0, 0), (0, 0)))
    decode = finish(block_parts, got_q, own_vecs, own_new[:, 0], own_new[:, 1])
    return place(parts)[None], decode.reshape(ROW_GRP, 2, GROUP * HD)


def solution(mesh):
    return jax.shard_map(
        local,
        mesh=mesh,
        in_specs=(
            P("grp", "ctx", None),
            P("grp", "ctx", None),
            P("grp", "ctx", None, None),
            P("grp", "ctx", None),
            P("grp", None, None),
            P("grp", None, None),
            P("grp", "ctx", None),
            P("grp"),
        ),
        out_specs=(P("grp", "ctx", None), P("grp", None, "ctx")),
        check_vma=False,
    )
```

```python
import functools
import math

import jax
import jax.numpy as jnp
from jax import lax
from jax.experimental import pallas as pl
from jax.experimental.pallas import tpu as pltpu
from jax.sharding import PartitionSpec as P

HD = 128
KVH = 8
GROUP = 8
PRE_DEV = 496
TAIL_DEV = 64
BLK = 16
ROW_GRP = 4
RES_DEV = 128
KVD = 1024
SEQ_DEV = 560
N_CTX = 8
N_GRP = 16

KEYS = N_CTX * SEQ_DEV
TAIL = N_CTX * TAIL_DEV
Q_ROWS = GROUP * TAIL_DEV
SEND_ROWS = SEQ_DEV + 16
VECS = 2 * GROUP
OWN_VECS = ROW_GRP * VECS
PART_ROWS = OWN_VECS + 16
QPART_ROWS = Q_ROWS + PART_ROWS
STEP = 2
ROWS_STEP = STEP * Q_ROWS
SPAN = 512
REST = SEQ_DEV - SPAN
BITS = (1, 4, 8, 2)

FLOOR = -1e30
LOG2E = 1.4426950408889634
COEF = LOG2E / math.sqrt(HD)
VMEM = 58 * 2**20
NT = (((1,), (1,)), ((), ()))


def widen_query(q):
    scaled = q.astype(jnp.float32) * COEF
    high = scaled.astype(jnp.bfloat16)
    low = (scaled - high.astype(jnp.float32)).astype(jnp.bfloat16)
    return jnp.concatenate([high, low], axis=1)


def part_of(acc, peak):
    rows = acc.shape[0]
    total = jnp.maximum(acc[:, HD:], 1.0)
    out = (acc[:, :HD] / total).astype(jnp.bfloat16)
    weight = peak + jnp.log2(total)
    diag = lax.broadcasted_iota(jnp.int32, (rows, HD), 0) == lax.broadcasted_iota(
        jnp.int32, (rows, HD), 1
    )
    line = jnp.sum(jnp.where(diag, weight, 0.0), axis=0, keepdims=True)
    first = line.astype(jnp.bfloat16)
    rest = line - first.astype(jnp.float32)
    second = rest.astype(jnp.bfloat16)
    third = rest - second.astype(jnp.float32)
    place = lax.broadcasted_iota(jnp.int32, (16, HD), 0)
    stats = jnp.where(
        place == 0,
        first.astype(jnp.float32),
        jnp.where(place == 1, second.astype(jnp.float32), jnp.where(place == 2, third, 0.0)),
    )
    return out, stats.astype(jnp.bfloat16)


def spans(total):
    return [(at, min(SPAN, total - at)) for at in range(0, total, SPAN)]


def whole(space=pltpu.VMEM):
    return pl.BlockSpec(memory_space=space)


def pack_kernel(
    owner_hbm, row_hbm, kv_ref, out_hbm, out_ref, owner_ref, row_ref, sems, small, done
):
    named = [
        pltpu.make_async_copy(owner_hbm, owner_ref, small.at[0]),
        pltpu.make_async_copy(row_hbm, row_ref, small.at[1]),
    ]
    for copy in named:
        copy.start()
    copies = []

    def add(src, dst):
        copies.append(pltpu.make_async_copy(src, dst, sems.at[len(copies)]))
        copies[-1].start()

    for e in range(KVH):
        for half in range(2):
            lanes = pl.ds(half * HD, HD)
            add(
                kv_ref.at[:, pl.ds(half * KVD + e * HD, HD)],
                out_ref.at[e, pl.ds(0, SEQ_DEV), lanes],
            )
    for copy in named:
        copy.wait()
    shape = (16, 2 * HD)
    place = lax.broadcasted_iota(jnp.int32, shape, 0) * (2 * HD)
    place += lax.broadcasted_iota(jnp.int32, shape, 1)
    rest = place - SPAN - lax.axis_index("ctx") * REST
    rest = jnp.where((rest >= 0) & (rest < REST), rest + SPAN, SEQ_DEV)
    block = jnp.where(place < SPAN, place, rest) // BLK
    labels = jnp.zeros(shape, jnp.float32)
    for b in range(SEQ_DEV // BLK):
        value = (owner_ref[b] * ROW_GRP + row_ref[b]).astype(jnp.float32)
        labels = jnp.where(block == b, value, labels)
    labels = labels.astype(jnp.bfloat16)
    for e in range(KVH):
        out_ref[e, SEQ_DEV:, :] = labels
    written = []
    for e in range(KVH):
        copies[2 * e].wait()
        copies[2 * e + 1].wait()
        written.append(pltpu.make_async_copy(out_ref.at[e], out_hbm.at[e], done.at[e]))
        written[-1].start()
    for copy in written:
        copy.wait()


def pack(owner, row, kv):
    return pl.pallas_call(
        pack_kernel,
        in_specs=[whole(pltpu.HBM)] * 3,
        out_specs=whole(pltpu.HBM),
        out_shape=jax.ShapeDtypeStruct((KVH, SEND_ROWS, 2 * HD), jnp.bfloat16),
        scratch_shapes=[
            pltpu.VMEM((KVH, SEND_ROWS, 2 * HD), jnp.bfloat16),
            pltpu.SMEM((SEQ_DEV // BLK,), jnp.int32),
            pltpu.SMEM((SEQ_DEV // BLK,), jnp.int32),
            pltpu.SemaphoreType.DMA((KVH * 2,)),
            pltpu.SemaphoreType.DMA((2,)),
            pltpu.SemaphoreType.DMA((KVH,)),
        ],
        compiler_params=pltpu.CompilerParams(vmem_limit_bytes=VMEM),
        cost_estimate=pl.CostEstimate(flops=0, bytes_accessed=4600000, transcendentals=0),
        name="pack",
    )(owner, row, kv)


def query_res_kernel(live_ref, q_ref, dq_ref, k_ref, v_ref, out_ref, vs_ref):
    for head in range(GROUP):
        out_ref[0, head * TAIL_DEV : (head + 1) * TAIL_DEV, :] = q_ref[
            :, head * HD : (head + 1) * HD
        ]
    keys = k_ref[...].reshape(ROW_GRP * RES_DEV, HD)
    vs_ref[:, :HD] = v_ref[...].reshape(ROW_GRP * RES_DEV, HD)
    vs_ref[:, HD:] = jnp.ones((ROW_GRP * RES_DEV, HD), jnp.bfloat16)
    query = widen_query(dq_ref[0])
    scores = lax.dot_general(query[:, :HD], keys, NT, preferred_element_type=jnp.float32)
    scores += lax.dot_general(query[:, HD:], keys, NT, preferred_element_type=jnp.float32)
    shape = (OWN_VECS, ROW_GRP * RES_DEV)
    row = lax.broadcasted_iota(jnp.int32, shape, 0)
    col = lax.broadcasted_iota(jnp.int32, shape, 1)
    for r in range(ROW_GRP):
        inside = (row >= r * VECS) & (row < (r + 1) * VECS)
        low, high = r * RES_DEV, jnp.clip(live_ref[r], 0, RES_DEV) + r * RES_DEV
        scores = jnp.where(inside & ((col < low) | (col >= high)), -jnp.inf, scores)
    peak = jnp.maximum(jnp.max(scores, axis=1, keepdims=True), FLOOR)
    weights = jnp.exp2(scores - peak).astype(jnp.bfloat16)
    acc = jnp.dot(weights, vs_ref[...], preferred_element_type=jnp.float32)
    out, stats = part_of(acc, peak)
    out_ref[0, Q_ROWS : Q_ROWS + OWN_VECS, :] = out
    out_ref[0, Q_ROWS + OWN_VECS :, :] = stats


def query_res(live, tail_q, dec_vecs, res_kv):
    return pl.pallas_call(
        query_res_kernel,
        grid=(KVH,),
        in_specs=[
            pl.BlockSpec(memory_space=pltpu.SMEM),
            pl.BlockSpec((TAIL_DEV, GROUP * HD), lambda e: (0, e)),
            pl.BlockSpec((1, OWN_VECS, HD), lambda e: (e, 0, 0)),
            pl.BlockSpec((ROW_GRP, RES_DEV, HD), lambda e: (0, 0, e)),
            pl.BlockSpec((ROW_GRP, RES_DEV, HD), lambda e: (0, 0, KVH + e)),
        ],
        out_specs=pl.BlockSpec((1, QPART_ROWS, HD), lambda e: (e, 0, 0)),
        out_shape=jax.ShapeDtypeStruct((KVH, QPART_ROWS, HD), jnp.bfloat16),
        scratch_shapes=[pltpu.VMEM((ROW_GRP * RES_DEV, 2 * HD), jnp.bfloat16)],
        cost_estimate=pl.CostEstimate(flops=500000000, bytes_accessed=4600000, transcendentals=0),
        name="query_res",
    )(live, tail_q, dec_vecs, res_kv, res_kv)


def attend(query, k_s, v_s, pieces, masker, ready=None):
    def score(at, n):
        if ready is not None:
            ready(at)
        scores = lax.dot_general(
            query, k_s[at : at + n, :], NT, preferred_element_type=jnp.float32
        )
        return masker(scores, at)

    peak = acc = None
    scores = score(*pieces[0])
    for i, (at, n) in enumerate(pieces):
        later = score(*pieces[i + 1]) if i + 1 < len(pieces) else None
        top = jnp.maximum(jnp.max(scores, axis=1, keepdims=True), FLOOR)
        new_peak = top if peak is None else jnp.maximum(peak, top)
        weights = jnp.exp2(scores - new_peak).astype(jnp.bfloat16)
        mixed = jnp.dot(weights, v_s[at : at + n, :], preferred_element_type=jnp.float32)
        acc = mixed if peak is None else acc * jnp.exp2(peak - new_peak) + mixed
        peak, scores = new_peak, later
    return peak, acc


def fetch(got_ref, got_s, sems):
    copies = [
        pltpu.make_async_copy(got_ref.at[s], got_s.at[s], sems.at[s]) for s in range(N_CTX)
    ]
    for copy in copies:
        copy.start()
    return copies


def fill(k_s, v_s, at, got_s, shard, src, n):
    keys = got_s[shard, src : src + n, :HD]
    k_s[at : at + n, :HD] = keys
    k_s[at : at + n, HD:] = keys
    v_s[at : at + n, :HD] = got_s[shard, src : src + n, HD:]


def shard_queries(got_ref, step):
    parts = [got_ref[step * STEP + g, :Q_ROWS, :] for g in range(STEP)]
    return widen_query(jnp.concatenate(parts, axis=0))


def blocks_kernel(got_ref, dq_ref, o_ref, k_s, v_s, got_s, sems):
    copies = fetch(got_ref, got_s, sems)
    v_s[:, HD:] = jnp.ones((KEYS, HD), jnp.bfloat16)

    def ready(at):
        first = at // SPAN
        if first < N_CTX:
            copies[first].wait()
            fill(k_s, v_s, at, got_s, first, 0, SPAN)
        else:
            for s in range(N_CTX):
                fill(k_s, v_s, at + s * REST, got_s, s, SPAN, REST)

    rows = dq_ref.shape[0]
    row = lax.broadcasted_iota(jnp.int32, (rows, 1), 0)
    place = row // OWN_VECS
    owner = jnp.zeros_like(place)
    for i, bit in enumerate(BITS):
        owner += (place // 2**i % 2) * bit
    row = (owner * ROW_GRP + row % OWN_VECS // VECS).astype(jnp.float32)

    def labels_of(s, first):
        pair = got_s[s, SEQ_DEV:, :].astype(jnp.float32)
        return jnp.concatenate([pair[first : first + 1], pair[first + 1 : first + 2]], axis=1)

    def masker(scores, at):
        if at // SPAN < N_CTX:
            labels = labels_of(at // SPAN, 0)
        else:
            labels = labels_of(0, 2)
            for s in range(1, N_CTX):
                labels += labels_of(s, 2)
            labels = labels[:, : N_CTX * REST]
        return jnp.where(labels == row, scores, -jnp.inf)

    peak, acc = attend(widen_query(dq_ref[...]), k_s, v_s, spans(KEYS), masker, ready)
    for place in range(rows // OWN_VECS):
        owner = sum((place >> i & 1) * bit for i, bit in enumerate(BITS))
        span = slice(place * OWN_VECS, (place + 1) * OWN_VECS)
        out, stats = part_of(acc[span], peak[span])
        o_ref[owner, :OWN_VECS, :] = out
        o_ref[owner, OWN_VECS:, :] = stats


def blocks(got, dec_vecs):
    return pl.pallas_call(
        blocks_kernel,
        in_specs=[whole(pltpu.HBM), whole()],
        out_specs=[whole()] * 3,
        out_shape=[
            jax.ShapeDtypeStruct((N_GRP, PART_ROWS, HD), jnp.bfloat16),
            jax.ShapeDtypeStruct((KEYS, 2 * HD), jnp.bfloat16),
            jax.ShapeDtypeStruct((KEYS, 2 * HD), jnp.bfloat16),
        ],
        scratch_shapes=[
            pltpu.VMEM((N_CTX, SEND_ROWS, 2 * HD), jnp.bfloat16),
            pltpu.SemaphoreType.DMA((N_CTX,)),
        ],
        compiler_params=pltpu.CompilerParams(vmem_limit_bytes=VMEM),
        cost_estimate=pl.CostEstimate(
            flops=8000000000, bytes_accessed=3000000, transcendentals=4700000
        ),
        name="blocks",
    )(got, dec_vecs)


def prefill_kernel(got_q_ref, k_s, v_s, o_ref):
    step = pl.program_id(0)
    row = lax.broadcasted_iota(jnp.int32, (ROWS_STEP, 1), 0)
    token = row % TAIL_DEV + (step * STEP + row // Q_ROWS) * TAIL_DEV

    def masker(scores, at):
        shard = at // SPAN
        if shard < N_CTX:
            col = lax.broadcasted_iota(jnp.int32, (1, HD), 1) - (HD - SPAN + PRE_DEV)
            place = jnp.where(col >= 0, col + shard * TAIL_DEV, -1)
            last = jnp.where(place > token, -jnp.inf, scores[:, SPAN - HD :])
            return jnp.concatenate([scores[:, : SPAN - HD], last], axis=1)
        col = lax.broadcasted_iota(jnp.int32, (1, N_CTX * REST), 1)
        place = col // REST * TAIL_DEV + (SPAN - PRE_DEV) + col % REST
        return jnp.where(place > token, -jnp.inf, scores)

    _, acc = attend(shard_queries(got_q_ref, 0), k_s, v_s, spans(KEYS), masker)
    out = (acc[:, :HD] / acc[:, HD:]).astype(jnp.bfloat16)
    for g in range(STEP):
        for head in range(GROUP):
            at = g * Q_ROWS + head * TAIL_DEV
            o_ref[g, :, head * HD : (head + 1) * HD] = out[at : at + TAIL_DEV]


def prefill(got_q, keys, values):
    return pl.pallas_call(
        prefill_kernel,
        grid=(N_CTX // STEP,),
        in_specs=[
            pl.BlockSpec((STEP, QPART_ROWS, HD), lambda i: (i, 0, 0)),
            whole(),
            whole(),
        ],
        out_specs=pl.BlockSpec((STEP, TAIL_DEV, GROUP * HD), lambda i: (i, 0, 0)),
        out_shape=jax.ShapeDtypeStruct((N_CTX, TAIL_DEV, GROUP * HD), jnp.bfloat16),
        compiler_params=pltpu.CompilerParams(vmem_limit_bytes=VMEM),
        cost_estimate=pl.CostEstimate(
            flops=26000000000, bytes_accessed=6000000, transcendentals=18000000
        ),
        name="prefill",
    )(got_q, keys, values)


def finish_kernel(blk_ref, in_ref, q_ref, nk_ref, nv_ref, o_ref):
    shape = (OWN_VECS, HD)
    row = lax.broadcasted_iota(jnp.int32, shape, 0)
    col = lax.broadcasted_iota(jnp.int32, shape, 1)
    diag = row == col
    query = widen_query(q_ref[...])
    keys = jnp.concatenate([nk_ref[...], jnp.zeros((HD - 16, HD), jnp.bfloat16)], axis=0)
    values = jnp.concatenate([nv_ref[...], jnp.zeros((HD - 16, HD), jnp.bfloat16)], axis=0)
    scores = lax.dot_general(query[:, :HD], keys, NT, preferred_element_type=jnp.float32)
    scores += lax.dot_general(query[:, HD:], keys, NT, preferred_element_type=jnp.float32)
    open_ = (col // 2 == row // VECS) & (col % 2 <= row % VECS // GROUP)
    scores = jnp.where(open_, scores, -jnp.inf)
    outs, weights = [], []
    parts = [(blk_ref[i, :OWN_VECS, :], blk_ref[i, OWN_VECS:, :]) for i in range(N_GRP)]
    for i in range(N_CTX):
        parts.append(
            (in_ref[i, Q_ROWS : Q_ROWS + OWN_VECS, :], in_ref[i, Q_ROWS + OWN_VECS :, :])
        )
    for out, stats in parts:
        outs.append(out)
        line = jnp.sum(stats.astype(jnp.float32)[:8], axis=0, keepdims=True)
        weights.append(jnp.sum(jnp.where(diag, line, 0.0), axis=1, keepdims=True))
    peak = jnp.max(scores, axis=1, keepdims=True)
    for weight in weights:
        peak = jnp.maximum(peak, weight)
    new = jnp.exp2(scores - peak)
    total = jnp.sum(new, axis=1, keepdims=True)
    mixed = jnp.dot(new.astype(jnp.bfloat16), values, preferred_element_type=jnp.float32)
    for out, weight in zip(outs, weights):
        share = jnp.exp2(weight - peak)
        total += share
        mixed += share * out.astype(jnp.float32)
    out = mixed / total
    for token in range(ROW_GRP * 2):
        for head in range(GROUP):
            at = token * GROUP + head
            o_ref[token : token + 1, head * HD : (head + 1) * HD] = out[at : at + 1].astype(
                jnp.bfloat16
            )


def finish(block_parts, got_q, queries, new_keys, new_values):
    return pl.pallas_call(
        finish_kernel,
        in_specs=[whole()] * 5,
        out_specs=whole(),
        out_shape=jax.ShapeDtypeStruct((ROW_GRP * 2, GROUP * HD), jnp.bfloat16),
        compiler_params=pltpu.CompilerParams(vmem_limit_bytes=16 * 2**20),
        cost_estimate=pl.CostEstimate(flops=5000000, bytes_accessed=1600000, transcendentals=0),
        name="finish",
    )(block_parts, got_q, queries, new_keys, new_values)


def place_kernel(in_ref, out_ref, sems):
    copies = []
    for e in range(KVH):
        lanes = pl.ds(e * GROUP * HD, GROUP * HD)
        copies.append(pltpu.make_async_copy(in_ref.at[e], out_ref.at[:, lanes], sems.at[e]))
        copies[-1].start()
    for copy in copies:
        copy.wait()


def place(parts):
    return pl.pallas_call(
        place_kernel,
        in_specs=[whole()],
        out_specs=whole(pl.ANY),
        out_shape=jax.ShapeDtypeStruct((TAIL_DEV, KVH * GROUP * HD), jnp.bfloat16),
        scratch_shapes=[pltpu.SemaphoreType.DMA((KVH,))],
        compiler_params=pltpu.CompilerParams(vmem_limit_bytes=8 * 2**20),
        cost_estimate=pl.CostEstimate(flops=0, bytes_accessed=2100000, transcendentals=0),
        name="place",
    )(parts)


def spread_over(values, axis, size, before, got):
    values = values + before[0, :1, :] * 0
    me = lax.axis_index(axis)
    for bit in BITS:
        if bit == BITS[-1]:
            values = values + got[0, :1, :HD] * 0
        other = lax.ppermute(values, axis, [(i, i ^ bit) for i in range(size)])
        upper = (me & bit) != 0
        values = jnp.concatenate(
            [jnp.where(upper, other, values), jnp.where(upper, values, other)], axis=0
        )
    return values


def local(tail_q, prompt_kv, dest_owner, dest_row, dec_q, new_kv, res_kv, lens):
    ctx = lax.axis_index("ctx")
    sent = pack(dest_owner.reshape(-1), dest_row.reshape(-1), prompt_kv[0])
    got = lax.all_to_all(sent, "ctx", split_axis=0, concat_axis=0, tiled=True)

    dec_vecs = dec_q.reshape(ROW_GRP * 2, KVH, GROUP, HD).transpose(1, 0, 2, 3)
    dec_vecs = dec_vecs.reshape(KVH, OWN_VECS, HD)
    own_vecs = lax.dynamic_index_in_dim(dec_vecs, ctx, 0, keepdims=False)
    sent_q = query_res(lens - ctx * RES_DEV, tail_q[0], dec_vecs, res_kv)
    got_q = lax.all_to_all(sent_q, "ctx", split_axis=0, concat_axis=0, tiled=True)
    all_vecs = spread_over(own_vecs, "grp", N_GRP, sent_q, got)

    block_parts, keys, values = blocks(got, all_vecs)
    block_parts = lax.all_to_all(block_parts, "grp", split_axis=0, concat_axis=0, tiled=True)
    parts = prefill(got_q, keys, values)
    parts = lax.all_to_all(parts, "ctx", split_axis=0, concat_axis=0, tiled=True)

    own_new = new_kv.reshape(ROW_GRP * 2, 2, KVH, HD)
    own_new = lax.dynamic_index_in_dim(own_new, ctx, 2, keepdims=False)
    own_new = jnp.pad(own_new, ((0, 8), (0, 0), (0, 0)))
    decode = finish(block_parts, got_q, own_vecs, own_new[:, 0], own_new[:, 1])
    return place(parts)[None], decode.reshape(ROW_GRP, 2, GROUP * HD)


def solution(mesh):
    return jax.shard_map(
        local,
        mesh=mesh,
        in_specs=(
            P("grp", "ctx", None),
            P("grp", "ctx", None),
            P("grp", "ctx", None, None),
            P("grp", "ctx", None),
            P("grp", None, None),
            P("grp", None, None),
            P("grp", "ctx", None),
            P("grp"),
        ),
        out_specs=(P("grp", "ctx", None), P("grp", None, "ctx")),
        check_vma=False,
    )
```

```python
import functools
import math

import jax
import jax.numpy as jnp
from jax import lax
from jax.experimental import pallas as pl
from jax.experimental.pallas import tpu as pltpu
from jax.sharding import PartitionSpec as P

HD = 128
KVH = 8
GROUP = 8
PRE_DEV = 496
TAIL_DEV = 64
BLK = 16
ROW_GRP = 4
RES_DEV = 128
KVD = 1024
SEQ_DEV = 560
N_CTX = 8
N_GRP = 16

KEYS = N_CTX * SEQ_DEV
TAIL = N_CTX * TAIL_DEV
Q_ROWS = GROUP * TAIL_DEV
SEND_ROWS = SEQ_DEV + 16
VECS = 2 * GROUP
OWN_VECS = ROW_GRP * VECS
PART_ROWS = OWN_VECS + 16
QPART_ROWS = Q_ROWS + PART_ROWS
STEP = 2
ROWS_STEP = STEP * Q_ROWS
SPAN = 512
REST = SEQ_DEV - SPAN
BITS = (1, 4, 8, 2)

FLOOR = -1e30
LOG2E = 1.4426950408889634
COEF = LOG2E / math.sqrt(HD)
VMEM = 58 * 2**20
NT = (((1,), (1,)), ((), ()))


def widen_query(q):
    scaled = q.astype(jnp.float32) * COEF
    high = scaled.astype(jnp.bfloat16)
    low = (scaled - high.astype(jnp.float32)).astype(jnp.bfloat16)
    return jnp.concatenate([high, low], axis=1)


def part_of(acc, peak):
    rows = acc.shape[0]
    total = jnp.maximum(acc[:, HD:], 1.0)
    out = (acc[:, :HD] / total).astype(jnp.bfloat16)
    weight = peak + jnp.log2(total)
    diag = lax.broadcasted_iota(jnp.int32, (rows, HD), 0) == lax.broadcasted_iota(
        jnp.int32, (rows, HD), 1
    )
    line = jnp.sum(jnp.where(diag, weight, 0.0), axis=0, keepdims=True)
    first = line.astype(jnp.bfloat16)
    rest = line - first.astype(jnp.float32)
    second = rest.astype(jnp.bfloat16)
    third = rest - second.astype(jnp.float32)
    place = lax.broadcasted_iota(jnp.int32, (16, HD), 0)
    stats = jnp.where(
        place == 0,
        first.astype(jnp.float32),
        jnp.where(place == 1, second.astype(jnp.float32), jnp.where(place == 2, third, 0.0)),
    )
    return out, stats.astype(jnp.bfloat16)


def spans(total):
    return [(at, min(SPAN, total - at)) for at in range(0, total, SPAN)]


def whole(space=pltpu.VMEM):
    return pl.BlockSpec(memory_space=space)


def pack_kernel(
    owner_hbm, row_hbm, kv_ref, out_hbm, out_ref, owner_ref, row_ref, sems, small, done
):
    named = [
        pltpu.make_async_copy(owner_hbm, owner_ref, small.at[0]),
        pltpu.make_async_copy(row_hbm, row_ref, small.at[1]),
    ]
    for copy in named:
        copy.start()
    copies = []

    def add(src, dst):
        copies.append(pltpu.make_async_copy(src, dst, sems.at[len(copies)]))
        copies[-1].start()

    for e in range(KVH):
        for half in range(2):
            lanes = pl.ds(half * HD, HD)
            add(
                kv_ref.at[:, pl.ds(half * KVD + e * HD, HD)],
                out_ref.at[e, pl.ds(0, SEQ_DEV), lanes],
            )
    for copy in named:
        copy.wait()
    shape = (16, 2 * HD)
    place = lax.broadcasted_iota(jnp.int32, shape, 0) * (2 * HD)
    place += lax.broadcasted_iota(jnp.int32, shape, 1)
    rest = place - SPAN - lax.axis_index("ctx") * REST
    rest = jnp.where((rest >= 0) & (rest < REST), rest + SPAN, SEQ_DEV)
    block = jnp.where(place < SPAN, place, rest) // BLK
    labels = jnp.zeros(shape, jnp.float32)
    for b in range(SEQ_DEV // BLK):
        value = (owner_ref[b] * ROW_GRP + row_ref[b]).astype(jnp.float32)
        labels = jnp.where(block == b, value, labels)
    labels = labels.astype(jnp.bfloat16)
    for e in range(KVH):
        out_ref[e, SEQ_DEV:, :] = labels
    written = []
    for e in range(KVH):
        copies[2 * e].wait()
        copies[2 * e + 1].wait()
        written.append(pltpu.make_async_copy(out_ref.at[e], out_hbm.at[e], done.at[e]))
        written[-1].start()
    for copy in written:
        copy.wait()


def pack(owner, row, kv):
    return pl.pallas_call(
        pack_kernel,
        in_specs=[whole(pltpu.HBM)] * 3,
        out_specs=whole(pltpu.HBM),
        out_shape=jax.ShapeDtypeStruct((KVH, SEND_ROWS, 2 * HD), jnp.bfloat16),
        scratch_shapes=[
            pltpu.VMEM((KVH, SEND_ROWS, 2 * HD), jnp.bfloat16),
            pltpu.SMEM((SEQ_DEV // BLK,), jnp.int32),
            pltpu.SMEM((SEQ_DEV // BLK,), jnp.int32),
            pltpu.SemaphoreType.DMA((KVH * 2,)),
            pltpu.SemaphoreType.DMA((2,)),
            pltpu.SemaphoreType.DMA((KVH,)),
        ],
        compiler_params=pltpu.CompilerParams(vmem_limit_bytes=VMEM),
        cost_estimate=pl.CostEstimate(flops=0, bytes_accessed=4600000, transcendentals=0),
        name="pack",
    )(owner, row, kv)


def query_res_kernel(live_ref, q_ref, dq_ref, k_ref, v_ref, out_ref, vs_ref):
    for head in range(GROUP):
        out_ref[0, head * TAIL_DEV : (head + 1) * TAIL_DEV, :] = q_ref[
            :, head * HD : (head + 1) * HD
        ]
    keys = k_ref[...].reshape(ROW_GRP * RES_DEV, HD)
    vs_ref[:, :HD] = v_ref[...].reshape(ROW_GRP * RES_DEV, HD)
    vs_ref[:, HD:] = jnp.ones((ROW_GRP * RES_DEV, HD), jnp.bfloat16)
    query = widen_query(dq_ref[0])
    scores = lax.dot_general(query[:, :HD], keys, NT, preferred_element_type=jnp.float32)
    scores += lax.dot_general(query[:, HD:], keys, NT, preferred_element_type=jnp.float32)
    shape = (OWN_VECS, ROW_GRP * RES_DEV)
    row = lax.broadcasted_iota(jnp.int32, shape, 0)
    col = lax.broadcasted_iota(jnp.int32, shape, 1)
    for r in range(ROW_GRP):
        inside = (row >= r * VECS) & (row < (r + 1) * VECS)
        low, high = r * RES_DEV, jnp.clip(live_ref[r], 0, RES_DEV) + r * RES_DEV
        scores = jnp.where(inside & ((col < low) | (col >= high)), -jnp.inf, scores)
    peak = jnp.maximum(jnp.max(scores, axis=1, keepdims=True), FLOOR)
    weights = jnp.exp2(scores - peak).astype(jnp.bfloat16)
    acc = jnp.dot(weights, vs_ref[...], preferred_element_type=jnp.float32)
    out, stats = part_of(acc, peak)
    out_ref[0, Q_ROWS : Q_ROWS + OWN_VECS, :] = out
    out_ref[0, Q_ROWS + OWN_VECS :, :] = stats


def query_res(live, tail_q, dec_vecs, res_kv):
    return pl.pallas_call(
        query_res_kernel,
        grid=(KVH,),
        in_specs=[
            pl.BlockSpec(memory_space=pltpu.SMEM),
            pl.BlockSpec((TAIL_DEV, GROUP * HD), lambda e: (0, e)),
            pl.BlockSpec((1, OWN_VECS, HD), lambda e: (e, 0, 0)),
            pl.BlockSpec((ROW_GRP, RES_DEV, HD), lambda e: (0, 0, e)),
            pl.BlockSpec((ROW_GRP, RES_DEV, HD), lambda e: (0, 0, KVH + e)),
        ],
        out_specs=pl.BlockSpec((1, QPART_ROWS, HD), lambda e: (e, 0, 0)),
        out_shape=jax.ShapeDtypeStruct((KVH, QPART_ROWS, HD), jnp.bfloat16),
        scratch_shapes=[pltpu.VMEM((ROW_GRP * RES_DEV, 2 * HD), jnp.bfloat16)],
        cost_estimate=pl.CostEstimate(flops=500000000, bytes_accessed=4600000, transcendentals=0),
        name="query_res",
    )(live, tail_q, dec_vecs, res_kv, res_kv)


def attend(query, k_s, v_s, pieces, masker, ready=None):
    def score(at, n):
        if ready is not None:
            ready(at)
        scores = lax.dot_general(
            query, k_s[at : at + n, :], NT, preferred_element_type=jnp.float32
        )
        return masker(scores, at)

    peak = acc = None
    scores = score(*pieces[0])
    for i, (at, n) in enumerate(pieces):
        later = score(*pieces[i + 1]) if i + 1 < len(pieces) else None
        top = jnp.maximum(jnp.max(scores, axis=1, keepdims=True), FLOOR)
        new_peak = top if peak is None else jnp.maximum(peak, top)
        weights = jnp.exp2(scores - new_peak).astype(jnp.bfloat16)
        mixed = jnp.dot(weights, v_s[at : at + n, :], preferred_element_type=jnp.float32)
        acc = mixed if peak is None else acc * jnp.exp2(peak - new_peak) + mixed
        peak, scores = new_peak, later
    return peak, acc


def fetch(got_ref, got_s, sems):
    copies = [
        pltpu.make_async_copy(got_ref.at[s], got_s.at[s], sems.at[s]) for s in range(N_CTX)
    ]
    for copy in copies:
        copy.start()
    return copies


def fill(k_s, v_s, at, got_s, shard, src, n):
    keys = got_s[shard, src : src + n, :HD]
    k_s[at : at + n, :HD] = keys
    k_s[at : at + n, HD:] = keys
    v_s[at : at + n, :HD] = got_s[shard, src : src + n, HD:]


def shard_queries(got_ref, step):
    parts = [got_ref[step * STEP + g, :Q_ROWS, :] for g in range(STEP)]
    return widen_query(jnp.concatenate(parts, axis=0))


def blocks_kernel(got_ref, dq_ref, o_ref, k_s, v_s, got_s, sems):
    copies = fetch(got_ref, got_s, sems)
    v_s[:, HD:] = jnp.ones((KEYS, HD), jnp.bfloat16)

    def ready(at):
        first = at // SPAN
        if first < N_CTX:
            copies[first].wait()
            fill(k_s, v_s, at, got_s, first, 0, SPAN)
        else:
            for s in range(N_CTX):
                fill(k_s, v_s, at + s * REST, got_s, s, SPAN, REST)

    rows = dq_ref.shape[0]
    row = lax.broadcasted_iota(jnp.int32, (rows, 1), 0)
    place = row // OWN_VECS
    owner = jnp.zeros_like(place)
    for i, bit in enumerate(BITS):
        owner += (place // 2**i % 2) * bit
    row = (owner * ROW_GRP + row % OWN_VECS // VECS).astype(jnp.float32)

    def labels_of(s, first):
        pair = got_s[s, SEQ_DEV:, :].astype(jnp.float32)
        return jnp.concatenate([pair[first : first + 1], pair[first + 1 : first + 2]], axis=1)

    def masker(scores, at):
        if at // SPAN < N_CTX:
            labels = labels_of(at // SPAN, 0)
        else:
            labels = labels_of(0, 2)
            for s in range(1, N_CTX):
                labels += labels_of(s, 2)
            labels = labels[:, : N_CTX * REST]
        return jnp.where(labels == row, scores, -jnp.inf)

    peak, acc = attend(widen_query(dq_ref[...]), k_s, v_s, spans(KEYS), masker, ready)
    for place in range(rows // OWN_VECS):
        owner = sum((place >> i & 1) * bit for i, bit in enumerate(BITS))
        span = slice(place * OWN_VECS, (place + 1) * OWN_VECS)
        out, stats = part_of(acc[span], peak[span])
        o_ref[owner, :OWN_VECS, :] = out
        o_ref[owner, OWN_VECS:, :] = stats


def blocks(got, dec_vecs):
    return pl.pallas_call(
        blocks_kernel,
        in_specs=[whole(pltpu.HBM), whole()],
        out_specs=[whole()] * 3,
        out_shape=[
            jax.ShapeDtypeStruct((N_GRP, PART_ROWS, HD), jnp.bfloat16),
            jax.ShapeDtypeStruct((KEYS, 2 * HD), jnp.bfloat16),
            jax.ShapeDtypeStruct((KEYS, 2 * HD), jnp.bfloat16),
        ],
        scratch_shapes=[
            pltpu.VMEM((N_CTX, SEND_ROWS, 2 * HD), jnp.bfloat16),
            pltpu.SemaphoreType.DMA((N_CTX,)),
        ],
        compiler_params=pltpu.CompilerParams(vmem_limit_bytes=VMEM),
        cost_estimate=pl.CostEstimate(
            flops=8000000000, bytes_accessed=3000000, transcendentals=4700000
        ),
        name="blocks",
    )(got, dec_vecs)


def prefill_kernel(got_q_ref, k_s, v_s, o_ref):
    step = pl.program_id(0)
    row = lax.broadcasted_iota(jnp.int32, (ROWS_STEP, 1), 0)
    token = row % TAIL_DEV + (step * STEP + row // Q_ROWS) * TAIL_DEV

    def masker(scores, at):
        shard = at // SPAN
        if shard < N_CTX:
            col = lax.broadcasted_iota(jnp.int32, (1, HD), 1) - (HD - SPAN + PRE_DEV)
            place = jnp.where(col >= 0, col + shard * TAIL_DEV, -1)
            last = jnp.where(place > token, -jnp.inf, scores[:, SPAN - HD :])
            return jnp.concatenate([scores[:, : SPAN - HD], last], axis=1)
        col = lax.broadcasted_iota(jnp.int32, (1, N_CTX * REST), 1)
        place = col // REST * TAIL_DEV + (SPAN - PRE_DEV) + col % REST
        return jnp.where(place > token, -jnp.inf, scores)

    _, acc = attend(shard_queries(got_q_ref, 0), k_s, v_s, spans(KEYS), masker)
    out = (acc[:, :HD] / acc[:, HD:]).astype(jnp.bfloat16)
    for g in range(STEP):
        for head in range(GROUP):
            at = g * Q_ROWS + head * TAIL_DEV
            o_ref[g, :, head * HD : (head + 1) * HD] = out[at : at + TAIL_DEV]


def prefill(got_q, keys, values):
    return pl.pallas_call(
        prefill_kernel,
        grid=(N_CTX // STEP,),
        in_specs=[
            pl.BlockSpec((STEP, QPART_ROWS, HD), lambda i: (i, 0, 0)),
            whole(),
            whole(),
        ],
        out_specs=pl.BlockSpec((STEP, TAIL_DEV, GROUP * HD), lambda i: (i, 0, 0)),
        out_shape=jax.ShapeDtypeStruct((N_CTX, TAIL_DEV, GROUP * HD), jnp.bfloat16),
        compiler_params=pltpu.CompilerParams(vmem_limit_bytes=VMEM),
        cost_estimate=pl.CostEstimate(
            flops=26000000000, bytes_accessed=6000000, transcendentals=18000000
        ),
        name="prefill",
    )(got_q, keys, values)


def finish_kernel(blk_ref, in_ref, q_ref, nk_ref, nv_ref, o_ref):
    shape = (OWN_VECS, HD)
    row = lax.broadcasted_iota(jnp.int32, shape, 0)
    col = lax.broadcasted_iota(jnp.int32, shape, 1)
    diag = row == col
    query = widen_query(q_ref[...])
    keys = jnp.concatenate([nk_ref[...], jnp.zeros((HD - 16, HD), jnp.bfloat16)], axis=0)
    values = jnp.concatenate([nv_ref[...], jnp.zeros((HD - 16, HD), jnp.bfloat16)], axis=0)
    scores = lax.dot_general(query[:, :HD], keys, NT, preferred_element_type=jnp.float32)
    scores += lax.dot_general(query[:, HD:], keys, NT, preferred_element_type=jnp.float32)
    open_ = (col // 2 == row // VECS) & (col % 2 <= row % VECS // GROUP)
    scores = jnp.where(open_, scores, -jnp.inf)
    outs, weights = [], []
    parts = [(blk_ref[i, :OWN_VECS, :], blk_ref[i, OWN_VECS:, :]) for i in range(N_GRP)]
    for i in range(N_CTX):
        parts.append(
            (in_ref[i, Q_ROWS : Q_ROWS + OWN_VECS, :], in_ref[i, Q_ROWS + OWN_VECS :, :])
        )
    for out, stats in parts:
        outs.append(out)
        line = jnp.sum(stats.astype(jnp.float32)[:8], axis=0, keepdims=True)
        weights.append(jnp.sum(jnp.where(diag, line, 0.0), axis=1, keepdims=True))
    peak = jnp.max(scores, axis=1, keepdims=True)
    for weight in weights:
        peak = jnp.maximum(peak, weight)
    new = jnp.exp2(scores - peak)
    total = jnp.sum(new, axis=1, keepdims=True)
    mixed = jnp.dot(new.astype(jnp.bfloat16), values, preferred_element_type=jnp.float32)
    for out, weight in zip(outs, weights):
        share = jnp.exp2(weight - peak)
        total += share
        mixed += share * out.astype(jnp.float32)
    out = mixed / total
    for token in range(ROW_GRP * 2):
        for head in range(GROUP):
            at = token * GROUP + head
            o_ref[token : token + 1, head * HD : (head + 1) * HD] = out[at : at + 1].astype(
                jnp.bfloat16
            )


def finish(block_parts, got_q, queries, new_keys, new_values):
    return pl.pallas_call(
        finish_kernel,
        in_specs=[whole()] * 5,
        out_specs=whole(),
        out_shape=jax.ShapeDtypeStruct((ROW_GRP * 2, GROUP * HD), jnp.bfloat16),
        compiler_params=pltpu.CompilerParams(vmem_limit_bytes=16 * 2**20),
        cost_estimate=pl.CostEstimate(flops=5000000, bytes_accessed=1600000, transcendentals=0),
        name="finish",
    )(block_parts, got_q, queries, new_keys, new_values)


def place_kernel(in_ref, out_ref, sems):
    copies = []
    for e in range(KVH):
        lanes = pl.ds(e * GROUP * HD, GROUP * HD)
        copies.append(pltpu.make_async_copy(in_ref.at[e], out_ref.at[:, lanes], sems.at[e]))
        copies[-1].start()
    for copy in copies:
        copy.wait()


def place(parts):
    return pl.pallas_call(
        place_kernel,
        in_specs=[whole()],
        out_specs=whole(pl.ANY),
        out_shape=jax.ShapeDtypeStruct((TAIL_DEV, KVH * GROUP * HD), jnp.bfloat16),
        scratch_shapes=[pltpu.SemaphoreType.DMA((KVH,))],
        compiler_params=pltpu.CompilerParams(vmem_limit_bytes=8 * 2**20),
        cost_estimate=pl.CostEstimate(flops=0, bytes_accessed=2100000, transcendentals=0),
        name="place",
    )(parts)


def spread_over(values, axis, size, before):
    values = values + before[0, :1, :] * 0
    me = lax.axis_index(axis)
    for bit in BITS:
        other = lax.ppermute(values, axis, [(i, i ^ bit) for i in range(size)])
        upper = (me & bit) != 0
        values = jnp.concatenate(
            [jnp.where(upper, other, values), jnp.where(upper, values, other)], axis=0
        )
    return values


def local(tail_q, prompt_kv, dest_owner, dest_row, dec_q, new_kv, res_kv, lens):
    ctx = lax.axis_index("ctx")
    sent = pack(dest_owner.reshape(-1), dest_row.reshape(-1), prompt_kv[0])
    got = lax.all_to_all(sent, "ctx", split_axis=0, concat_axis=0, tiled=True)

    dec_vecs = dec_q.reshape(ROW_GRP * 2, KVH, GROUP, HD).transpose(1, 0, 2, 3)
    dec_vecs = dec_vecs.reshape(KVH, OWN_VECS, HD)
    own_vecs = lax.dynamic_index_in_dim(dec_vecs, ctx, 0, keepdims=False)
    sent_q = query_res(lens - ctx * RES_DEV, tail_q[0], dec_vecs, res_kv)
    got_q = lax.all_to_all(sent_q, "ctx", split_axis=0, concat_axis=0, tiled=True)
    all_vecs = spread_over(own_vecs, "grp", N_GRP, sent_q)

    block_parts, keys, values = blocks(got, all_vecs)
    block_parts = lax.all_to_all(block_parts, "grp", split_axis=0, concat_axis=0, tiled=True)
    parts = prefill(got_q, keys, values)
    parts = lax.all_to_all(parts, "ctx", split_axis=0, concat_axis=0, tiled=True)

    own_new = new_kv.reshape(ROW_GRP * 2, 2, KVH, HD)
    own_new = lax.dynamic_index_in_dim(own_new, ctx, 2, keepdims=False)
    own_new = jnp.pad(own_new, ((0, 8), (0, 0), (0, 0)))
    decode = finish(block_parts, got_q, own_vecs, own_new[:, 0], own_new[:, 1])
    return place(parts)[None], decode.reshape(ROW_GRP, 2, GROUP * HD)


def solution(mesh):
    return jax.shard_map(
        local,
        mesh=mesh,
        in_specs=(
            P("grp", "ctx", None),
            P("grp", "ctx", None),
            P("grp", "ctx", None, None),
            P("grp", "ctx", None),
            P("grp", None, None),
            P("grp", None, None),
            P("grp", "ctx", None),
            P("grp"),
        ),
        out_specs=(P("grp", "ctx", None), P("grp", None, "ctx")),
        check_vma=False,
    )
```
